32 devices in a mesh: row: 8 (over y, x, core), col: 4 (over z).
Axes of the slice: x: 2, y: 2, z: 4, core: 2. Of those that a mesh axis runs over, the one named last changes fastest.
Arguments:
- tokens: bfloat16 [448, 8192], P('col', 'row'), may hold values from -6 to 6
- gate_weight: bfloat16 [8192, 26624], P('row', 'col'), may hold values from -0.0625 to 0.0625
- up_weight: bfloat16 [8192, 26624], P('row', 'col'), may hold values from -0.0625 to 0.0625
- down_weight: bfloat16 [26624, 8192], P('col', 'row'), may hold values from -0.0390625 to 0.0390625
- cotangent: bfloat16 [448, 8192], P('col', 'row'), may hold values from -6 to 6
Outputs:
- layer_out: bfloat16 [448, 8192], P('col', 'row')
- token_grad: bfloat16 [448, 8192], P('col', 'row')
- gate_grad: bfloat16 [8192, 26624], P('row', 'col')
- up_grad: bfloat16 [8192, 26624], P('row', 'col')
- down_grad: bfloat16 [26624, 8192], P('col', 'row')
The draws below stay inside these ranges and needn't reach their ends.
All inputs are finite; a program needn't handle non-finite values.
Results may differ from the reference program's by a relative error of at most 0.0051.
Values may be sent and summed in bfloat16 or wider, within the bound.
A program may use at most 256 MiB of HBM per device.

```python
import jax
import jax.numpy as jnp
from jax import lax

D = 8192
FF = 26624
TOKENS = 448


def strengthened(drawn, own_key, source, target, shards_of, factor):
    owner, partner = [(jnp.arange(drawn.shape[position]) // (drawn.shape[position] // shards_of)).reshape([-1 if axis == position else 1 for axis in range(drawn.ndim)]) for position in (source, target)]
    chosen = jax.random.permutation(own_key, shards_of)[partner]
    strong = (owner == chosen) | (owner == (partner + shards_of // 2) % shards_of)
    return jnp.where(strong, factor * drawn, drawn)


def levels(own_key, extent, split, least, top_value):
    loudness = 1.0
    for dim, blocks in split:
        draws = jax.random.uniform(jax.random.fold_in(jax.random.fold_in(own_key, 6), dim), (blocks,), jnp.float32, least / len(split), top_value / len(split))
        loudness = loudness * jnp.repeat(jnp.exp(draws), extent[dim] // blocks).reshape((-1,) + (1,) * (len(extent) - 1 - dim))
    return loudness


def scatter_about(key, extent, scale, limit, shards=(), kind=jnp.bfloat16):
    level = levels(key, extent, shards, -0.22, 0.18) if shards else 1.0
    array = jax.random.normal(key, extent, jnp.float32) * scale * level
    return jnp.minimum(jnp.maximum(array, -limit), limit).astype(kind)


def bell_draw_with(own_key, shape, width, reach, shards, heavy, held_as=jnp.bfloat16):
    values = width * jax.random.normal(own_key, shape, jnp.float32)
    if shards:
        values = values * levels(own_key, shape, shards, -0.22, 0.18)
    return jnp.clip(strengthened(values, jax.random.fold_in(own_key, 3), *heavy), -reach, reach).astype(held_as)


def setup_inputs(seed: int = 0) -> dict:
    keys = jax.random.split(jax.random.key(seed), 6)
    tokens = bell_draw_with(keys[0], (TOKENS, D), 1.0, 6.0, ((0, 4), (1, 8)), (1, 0, 8, 2.0))
    gate_weight = scatter_about(keys[1], (D, FF), D ** -0.5, 0.0625, ((0, 8), (1, 4)))
    up_weight = scatter_about(keys[2], (D, FF), D ** -0.5, 0.0625, ((0, 8), (1, 4)))
    down_weight = scatter_about(keys[3], (FF, D), FF ** -0.5, 0.0390625, ((0, 4), (1, 8)))
    cotangent = scatter_about(keys[4], (TOKENS, D), 1.0, 6.0, ((0, 4), (1, 8)))
    return dict(tokens=tokens, gate_weight=gate_weight, up_weight=up_weight, down_weight=down_weight, cotangent=cotangent)


def reference(tokens, gate_weight, up_weight, down_weight, cotangent):
    gate_sum = jnp.dot(tokens, gate_weight, preferred_element_type=jnp.float32)
    up_sum = jnp.dot(tokens, up_weight, preferred_element_type=jnp.float32)
    sigmoid_gate = jax.nn.sigmoid(gate_sum)
    activated = gate_sum * sigmoid_gate
    hidden = (activated * up_sum).astype(jnp.bfloat16)
    layer_out = jnp.dot(hidden, down_weight, preferred_element_type=jnp.float32).astype(jnp.bfloat16)
    down_grad = lax.dot_general(hidden, cotangent, (((0,), (0,)), ((), ())), preferred_element_type=jnp.float32).astype(jnp.bfloat16)
    hidden_grad = lax.dot_general(cotangent, down_weight, (((1,), (1,)), ((), ())), preferred_element_type=jnp.float32)
    up_delta = (hidden_grad * activated).astype(jnp.bfloat16)
    gate_delta = (hidden_grad * up_sum * sigmoid_gate * (1.0 + gate_sum * (1.0 - sigmoid_gate))).astype(jnp.bfloat16)
    gate_grad = lax.dot_general(tokens, gate_delta, (((0,), (0,)), ((), ())), preferred_element_type=jnp.float32).astype(jnp.bfloat16)
    up_grad = lax.dot_general(tokens, up_delta, (((0,), (0,)), ((), ())), preferred_element_type=jnp.float32).astype(jnp.bfloat16)
    token_grad = lax.dot_general(gate_delta, gate_weight, (((1,), (1,)), ((), ())), preferred_element_type=jnp.float32)
    token_grad = token_grad + lax.dot_general(up_delta, up_weight, (((1,), (1,)), ((), ())), preferred_element_type=jnp.float32)
    return layer_out, token_grad.astype(jnp.bfloat16), gate_grad, up_grad, down_grad
```

```python
import jax
import jax.numpy as jnp
from jax import lax
from jax.sharding import PartitionSpec as P

F32, BF16 = jnp.float32, jnp.bfloat16


def contract(left, right, left_dim, right_dim):
    return lax.dot_general(
        left, right, (((left_dim,), (right_dim,)), ((), ())), preferred_element_type=F32
    )


def swap(value, size, bit):
    return lax.ppermute(value, "row", [(i, i ^ bit) for i in range(size)])


def gather_col(block, size):
    me = lax.axis_index("col")
    rows = block.shape[0]
    out = jnp.zeros((size * rows, block.shape[1]), block.dtype)
    out = lax.dynamic_update_slice(out, block, (me * rows, 0))
    for shift in range(1, size):
        got = lax.ppermute(block, "col", [(i, (i + shift) % size) for i in range(size)])
        out = lax.dynamic_update_slice(out, got, (((me - shift + size) % size) * rows, 0))
    return out


def reorder(value, size, me):
    blocks = value.reshape(size, -1, value.shape[1])
    index = jnp.arange(size) ^ me
    return jnp.take(blocks, index, axis=0, mode="clip").reshape(value.shape)


def make_body(rows, cols):
    bits = rows.bit_length() - 1
    link_bits = list(range(1, bits))

    def body(tokens, gate_weight, up_weight, down_weight, cotangent):
        me = lax.axis_index("row")
        all_cotangent = reorder(gather_col(cotangent, cols), rows, me)
        all_tokens = reorder(gather_col(tokens, cols), rows, me)
        units = gate_weight.shape[1]
        half = units // 2
        spans = ((0, half), (half, units))
        count = all_tokens.shape[0]
        small = count // rows

        def split_core(value):
            v = value.reshape(rows // 2, 2, small, value.shape[1])
            return [v[:, i].reshape(count // 2, value.shape[1]) for i in range(2)]

        tok_keep, tok_send = split_core(all_tokens)
        cot_keep, cot_send = split_core(all_cotangent)
        tok_all = jnp.concatenate([tok_keep, tok_send], 0)
        cot_all = jnp.concatenate([cot_keep, cot_send], 0)

        def scatter(product, which):
            got = swap(product(1).astype(BF16), rows, 1)
            total = product(0) + got.astype(F32)
            width = total.shape[1]
            shape = [2] * (bits - 1)
            total = total.reshape(shape + [small, width])
            live = list(reversed(link_bits))
            order = list(live) if which == 0 else list(reversed(live))
            for bit in order:
                axis = live.index(bit)
                send = lax.index_in_dim(total, 1, axis, keepdims=False).astype(BF16)
                keep = lax.index_in_dim(total, 0, axis, keepdims=False)
                total = keep + swap(send, rows, 1 << bit).astype(F32)
                live.remove(bit)
            return total

        def gather(block, which):
            total = block
            full = list(reversed(link_bits))
            order = full if which == 0 else list(reversed(full))
            live = []
            for bit in reversed(order):
                got = swap(total, rows, 1 << bit)
                live = sorted(live + [bit], reverse=True)
                total = jnp.stack([total, got], axis=live.index(bit))
            total = total.reshape(count // 2, block.shape[1])
            return jnp.concatenate([total, swap(total, rows, 1)], 0)

        parts_cot, parts_tok = (cot_keep, cot_send), (tok_keep, tok_send)
        hid = [
            scatter(lambda c: contract(parts_cot[c], down_weight[a:b], 1, 1), i)
            for i, (a, b) in enumerate(spans)
        ]
        gate = [
            scatter(lambda c: jnp.dot(parts_tok[c], gate_weight[:, a:b], preferred_element_type=F32), i)
            for i, (a, b) in enumerate(spans)
        ]
        up = [
            scatter(lambda c: jnp.dot(parts_tok[c], up_weight[:, a:b], preferred_element_type=F32), i)
            for i, (a, b) in enumerate(spans)
        ]
        hidden, gate_delta, up_delta = [], [], []
        for i in range(2):
            sigmoid_gate = jax.nn.sigmoid(gate[i])
            activated = gate[i] * sigmoid_gate
            hidden.append((activated * up[i]).astype(BF16))
            up_delta.append((hid[i] * activated).astype(BF16))
            gate_delta.append(
                (hid[i] * up[i] * sigmoid_gate * (1.0 + gate[i] * (1.0 - sigmoid_gate))).astype(BF16)
            )
        join = lambda blocks: jnp.concatenate([gather(b, i) for i, b in enumerate(blocks)], 1)
        tokens_t = lax.optimization_barrier(tok_all.T)
        gate_deltas = join(gate_delta)
        up_deltas = join(up_delta)
        hiddens = join(hidden)

        def to_global(value):
            keep, send = value[: count // 2], value[count // 2 :]
            both = jnp.stack(
                [x.reshape(rows // 2, small, x.shape[1]) for x in (keep, send)], 1
            ).reshape(value.shape)
            return reorder(both, rows, me)

        def finish(value):
            return lax.psum_scatter(
                to_global(value), "col", scatter_dimension=0, tiled=True
            ).astype(BF16)

        token_grad = finish(contract(gate_deltas, gate_weight, 1, 1) + contract(up_deltas, up_weight, 1, 1))
        gate_grad = jnp.dot(tokens_t, gate_deltas, preferred_element_type=F32).astype(BF16)
        up_grad = jnp.dot(tokens_t, up_deltas, preferred_element_type=F32).astype(BF16)
        layer_out = finish(jnp.dot(hiddens, down_weight, preferred_element_type=F32))
        down_grad = contract(hiddens, cot_all, 0, 0).astype(BF16)
        return (layer_out, token_grad, gate_grad, up_grad, down_grad)

    return body


def solution(mesh):
    placed = (P("col", "row"), P("row", "col"), P("row", "col"), P("col", "row"), P("col", "row"))
    return jax.shard_map(
        make_body(mesh.shape["row"], mesh.shape["col"]),
        mesh=mesh,
        in_specs=placed,
        out_specs=(
            P("col", "row"),
            P("col", "row"),
            P("row", "col"),
            P("row", "col"),
            P("col", "row"),
        ),
        check_vma=False,
    )
```

```python
import jax
import jax.numpy as jnp
from jax import lax
from jax.sharding import PartitionSpec as P

F32, BF16 = jnp.float32, jnp.bfloat16


def contract(left, right, left_dim, right_dim):
    return lax.dot_general(
        left, right, (((left_dim,), (right_dim,)), ((), ())), preferred_element_type=F32
    )


def swap(value, size, bit):
    return lax.ppermute(value, "row", [(i, i ^ bit) for i in range(size)])


def after(value, *earlier):
    for other in earlier:
        first = lax.slice(other, (0,) * other.ndim, (1,) * other.ndim).reshape(())
        value = value + (first.astype(F32) * 0.0).astype(value.dtype)
    return value


def scatter_col(share, size):
    me = lax.axis_index("col")
    rows = share.shape[0] // size
    part = lambda k: lax.dynamic_slice(share, (k % size * rows, 0), (rows, share.shape[1]))
    sent = [
        lax.ppermute(part(me + s).astype(BF16), "col", [(i, (i + s) % size) for i in range(size)])
        for s in range(1, size)
    ]
    total = part(me)
    for got in sent:
        total = total + got.astype(F32)
    return total.astype(BF16)


def gather_col(block, size):
    me = lax.axis_index("col")
    rows = block.shape[0]
    out = jnp.zeros((size * rows, block.shape[1]), block.dtype)
    out = lax.dynamic_update_slice(out, block, (me * rows, 0))
    for shift in range(1, size):
        got = lax.ppermute(block, "col", [(i, (i + shift) % size) for i in range(size)])
        out = lax.dynamic_update_slice(out, got, (((me - shift + size) % size) * rows, 0))
    return out


def reorder(value, size, me):
    blocks = value.reshape(size, -1, value.shape[1])
    index = jnp.arange(size) ^ me
    return jnp.take(blocks, index, axis=0, mode="clip").reshape(value.shape)


def make_body(rows, cols):
    bits = rows.bit_length() - 1
    link_bits = list(range(1, bits))

    def body(tokens, gate_weight, up_weight, down_weight, cotangent):
        me = lax.axis_index("row")
        col_tokens = gather_col(tokens, cols)
        all_tokens = reorder(col_tokens, rows, me)
        all_cotangent = reorder(gather_col(after(cotangent, col_tokens), cols), rows, me)
        units = gate_weight.shape[1]
        half = units // 2
        spans = ((0, half), (half, units))
        count = all_tokens.shape[0]
        small = count // rows

        def split_core(value):
            v = value.reshape(rows // 2, 2, small, value.shape[1])
            return [v[:, i].reshape(count // 2, value.shape[1]) for i in range(2)]

        tok_keep, tok_send = split_core(all_tokens)
        cot_keep, cot_send = split_core(all_cotangent)
        tok_all = jnp.concatenate([tok_keep, tok_send], 0)
        cot_all = jnp.concatenate([cot_keep, cot_send], 0)

        def scatter(total, which):
            width = total.shape[1]
            shape = [2] * (bits - 1)
            total = total.reshape(shape + [small, width])
            live = list(reversed(link_bits))
            order = list(live) if which == 0 else list(reversed(live))
            for bit in order:
                axis = live.index(bit)
                send = lax.index_in_dim(total, 1, axis, keepdims=False).astype(BF16)
                keep = lax.index_in_dim(total, 0, axis, keepdims=False)
                total = keep + swap(send, rows, 1 << bit).astype(F32)
                live.remove(bit)
            return total

        def gather(block, which, before_core):
            total = block
            full = list(reversed(link_bits))
            order = full if which == 0 else list(reversed(full))
            live = []
            for bit in reversed(order):
                got = swap(total, rows, 1 << bit)
                live = sorted(live + [bit], reverse=True)
                total = jnp.stack([total, got], axis=live.index(bit))
            total = after(total.reshape(count // 2, block.shape[1]), *before_core)
            return jnp.concatenate([total, swap(total, rows, 1)], 0), total

        def shares(left, weight, transposed):
            out = []
            for a, b in spans:
                if transposed:
                    out.append(contract(left, weight[a:b], 1, 1))
                else:
                    out.append(contract(left, weight[:, a:b], 1, 0))
            return out

        def cores(sends):
            return [swap(x, rows, 1) for x in sends]

        def sums(keeps, gots):
            return [scatter(k + g, i) for i, (k, g) in enumerate(zip(keeps, gots))]

        gate_send = shares(tok_send, gate_weight, False)
        gate_got = cores(gate_send)
        up_send = shares(after(tok_send, gate_send[1]), up_weight, False)
        up_got = cores(up_send)
        gate_keep = shares(after(tok_keep, up_send[1]), gate_weight, False)
        gate = sums(gate_keep, gate_got)
        hid_send = shares(after(cot_send, gate_keep[1]), down_weight, True)
        hid_got = cores(hid_send)
        up_keep = shares(after(tok_keep, hid_send[1]), up_weight, False)
        up = sums(up_keep, up_got)
        hidden, gate_delta, up_delta = [], [], []
        activated, slope = [], []
        for i in range(2):
            sigmoid_gate = jax.nn.sigmoid(gate[i])
            activated.append(gate[i] * sigmoid_gate)
            hidden.append((activated[i] * up[i]).astype(BF16))
            slope.append(up[i] * sigmoid_gate * (1.0 + gate[i] * (1.0 - sigmoid_gate)))
        hid_keep = shares(after(cot_keep, *hidden), down_weight, True)
        hid = sums(hid_keep, hid_got)
        for i in range(2):
            up_delta.append((hid[i] * activated[i]).astype(BF16))
            gate_delta.append((hid[i] * slope[i]).astype(BF16))

        def join(blocks, links_free, before_core, *earlier):
            both = [gather(after(b, *links_free), i, before_core) for i, b in enumerate(blocks)]
            return jnp.concatenate([after(x, *earlier) for x, _ in both], 1), [t for _, t in both]

        hiddens, _ = join(hidden, [], [], *hid_keep)
        tokens_t = lax.optimization_barrier(tok_all.T)
        out_share = jnp.dot(hiddens, down_weight, preferred_element_type=F32)
        down_grad = contract(hiddens, after(cot_all, out_share), 0, 0).astype(BF16)
        gate_deltas, gate_mid = join(gate_delta, [], [], down_grad)
        gate_grad = jnp.dot(tokens_t, gate_deltas, preferred_element_type=F32).astype(BF16)
        token_share = contract(after(gate_deltas, gate_grad), gate_weight, 1, 1)
        up_deltas, _ = join(up_delta, gate_mid, [gate_grad], token_share)
        token_share = token_share + contract(up_deltas, up_weight, 1, 1)
        up_grad = jnp.dot(
            after(tokens_t, token_share), up_deltas, preferred_element_type=F32
        ).astype(BF16)

        def to_global(value):
            keep, send = value[: count // 2], value[count // 2 :]
            both = jnp.stack(
                [x.reshape(rows // 2, small, x.shape[1]) for x in (keep, send)], 1
            ).reshape(value.shape)
            return reorder(both, rows, me)

        layer_out = scatter_col(to_global(out_share), cols)
        token_grad = scatter_col(to_global(token_share), cols)
        return (layer_out, token_grad, gate_grad, up_grad, down_grad)

    return body


def solution(mesh):
    placed = (P("col", "row"), P("row", "col"), P("row", "col"), P("col", "row"), P("col", "row"))
    return jax.shard_map(
        make_body(mesh.shape["row"], mesh.shape["col"]),
        mesh=mesh,
        in_specs=placed,
        out_specs=(
            P("col", "row"),
            P("col", "row"),
            P("row", "col"),
            P("row", "col"),
            P("col", "row"),
        ),
        check_vma=False,
    )
```

```python
import jax
import jax.numpy as jnp
from jax import lax
from jax.sharding import PartitionSpec as P

F32, BF16 = jnp.float32, jnp.bfloat16


def contract(left, right, left_dim, right_dim):
    return lax.dot_general(
        left, right, (((left_dim,), (right_dim,)), ((), ())), preferred_element_type=F32
    )


def swap(value, size, bit):
    return lax.ppermute(value, "row", [(i, i ^ bit) for i in range(size)])


def after(value, *earlier):
    for other in earlier:
        first = lax.slice(other, (0,) * other.ndim, (1,) * other.ndim).reshape(())
        value = value + (first.astype(F32) * 0.0).astype(value.dtype)
    return value


def scatter_col(share, size):
    me = lax.axis_index("col")
    rows = share.shape[0] // size
    part = lambda k: lax.dynamic_slice(share, (k % size * rows, 0), (rows, share.shape[1]))
    sent = [
        lax.ppermute(part(me + s).astype(BF16), "col", [(i, (i + s) % size) for i in range(size)])
        for s in range(1, size)
    ]
    total = part(me)
    for got in sent:
        total = total + got.astype(F32)
    return total.astype(BF16)


def gather_col(block, size):
    me = lax.axis_index("col")
    rows = block.shape[0]
    out = jnp.zeros((size * rows, block.shape[1]), block.dtype)
    out = lax.dynamic_update_slice(out, block, (me * rows, 0))
    for shift in range(1, size):
        got = lax.ppermute(block, "col", [(i, (i + shift) % size) for i in range(size)])
        out = lax.dynamic_update_slice(out, got, (((me - shift + size) % size) * rows, 0))
    return out


def reorder(value, size, me):
    blocks = value.reshape(size, -1, value.shape[1])
    index = jnp.arange(size) ^ me
    return jnp.take(blocks, index, axis=0, mode="clip").reshape(value.shape)


def make_body(rows, cols):
    bits = rows.bit_length() - 1
    link_bits = list(range(1, bits))

    def body(tokens, gate_weight, up_weight, down_weight, cotangent):
        me = lax.axis_index("row")
        col_tokens = gather_col(tokens, cols)
        all_tokens = reorder(col_tokens, rows, me)
        all_cotangent = reorder(gather_col(after(cotangent, col_tokens), cols), rows, me)
        units = gate_weight.shape[1]
        half = units // 2
        spans = ((0, half), (half, units))
        count = all_tokens.shape[0]
        small = count // rows

        def split_core(value):
            v = value.reshape(rows // 2, 2, small, value.shape[1])
            return [v[:, i].reshape(count // 2, value.shape[1]) for i in range(2)]

        tok_keep, tok_send = split_core(all_tokens)
        cot_keep, cot_send = split_core(all_cotangent)
        tok_all = jnp.concatenate([tok_keep, tok_send], 0)
        cot_all = jnp.concatenate([cot_keep, cot_send], 0)

        def scatter(total, which):
            width = total.shape[1]
            shape = [2] * (bits - 1)
            total = total.reshape(shape + [small, width])
            live = list(reversed(link_bits))
            order = list(live) if which == 0 else list(reversed(live))
            for bit in order:
                axis = live.index(bit)
                send = lax.index_in_dim(total, 1, axis, keepdims=False).astype(BF16)
                keep = lax.index_in_dim(total, 0, axis, keepdims=False)
                total = keep + swap(send, rows, 1 << bit).astype(F32)
                live.remove(bit)
            return total

        def gather(block, which, before_core):
            total = block
            full = list(reversed(link_bits))
            order = full if which == 0 else list(reversed(full))
            live = []
            for bit in reversed(order):
                got = swap(total, rows, 1 << bit)
                live = sorted(live + [bit], reverse=True)
                total = jnp.stack([total, got], axis=live.index(bit))
            total = after(total.reshape(count // 2, block.shape[1]), *before_core)
            return jnp.concatenate([total, swap(total, rows, 1)], 0), total

        def shares(left, weight, transposed):
            out = []
            for a, b in spans:
                if transposed:
                    out.append(contract(left, weight[a:b], 1, 1))
                else:
                    out.append(contract(left, weight[:, a:b], 1, 0))
            return out

        def cores(sends):
            return [swap(x, rows, 1) for x in sends]

        def sums(keeps, gots):
            return [scatter(k + g, i) for i, (k, g) in enumerate(zip(keeps, gots))]

        gate_send = shares(tok_send, gate_weight, False)
        gate_got = cores(gate_send)
        up_send = shares(after(tok_send, gate_send[1]), up_weight, False)
        up_got = cores(up_send)
        gate_keep = shares(after(tok_keep, up_send[1]), gate_weight, False)
        gate = sums(gate_keep, gate_got)
        hid_send = shares(after(cot_send, gate_keep[1]), down_weight, True)
        hid_got = cores(hid_send)
        up_keep = shares(after(tok_keep, hid_send[1]), up_weight, False)
        up = sums(up_keep, up_got)
        hid_keep = shares(after(cot_keep, up_keep[1]), down_weight, True)
        hid = sums(hid_keep, hid_got)
        hidden, gate_delta, up_delta = [], [], []
        activated, slope = [], []
        for i in range(2):
            sigmoid_gate = jax.nn.sigmoid(gate[i])
            activated.append(gate[i] * sigmoid_gate)
            hidden.append((activated[i] * up[i]).astype(BF16))
            slope.append(up[i] * sigmoid_gate * (1.0 + gate[i] * (1.0 - sigmoid_gate)))
        for i in range(2):
            up_delta.append((hid[i] * activated[i]).astype(BF16))
            gate_delta.append((hid[i] * slope[i]).astype(BF16))

        def join(blocks, links_free, before_core, *earlier):
            both = [gather(after(b, *links_free), i, before_core) for i, b in enumerate(blocks)]
            return jnp.concatenate([after(x, *earlier) for x, _ in both], 1), [t for _, t in both]

        hiddens, _ = join(hidden, [], [], *gate_delta)
        tokens_t = lax.optimization_barrier(tok_all.T)
        out_share = jnp.dot(hiddens, down_weight, preferred_element_type=F32)
        down_grad = contract(hiddens, after(cot_all, out_share), 0, 0).astype(BF16)
        gate_deltas, gate_mid = join(gate_delta, [], [down_grad])
        gate_grad = jnp.dot(tokens_t, gate_deltas, preferred_element_type=F32).astype(BF16)
        token_share = contract(after(gate_deltas, gate_grad), gate_weight, 1, 1)
        up_deltas, _ = join(up_delta, gate_mid, [gate_grad], token_share)
        token_share = token_share + contract(up_deltas, up_weight, 1, 1)
        up_grad = jnp.dot(
            after(tokens_t, token_share), up_deltas, preferred_element_type=F32
        ).astype(BF16)

        def to_global(value):
            keep, send = value[: count // 2], value[count // 2 :]
            both = jnp.stack(
                [x.reshape(rows // 2, small, x.shape[1]) for x in (keep, send)], 1
            ).reshape(value.shape)
            return reorder(both, rows, me)

        layer_out = scatter_col(to_global(out_share), cols)
        token_grad = scatter_col(to_global(token_share), cols)
        return (layer_out, token_grad, gate_grad, up_grad, down_grad)

    return body


def solution(mesh):
    placed = (P("col", "row"), P("row", "col"), P("row", "col"), P("col", "row"), P("col", "row"))
    return jax.shard_map(
        make_body(mesh.shape["row"], mesh.shape["col"]),
        mesh=mesh,
        in_specs=placed,
        out_specs=(
            P("col", "row"),
            P("col", "row"),
            P("row", "col"),
            P("row", "col"),
            P("col", "row"),
        ),
        check_vma=False,
    )
```
